32 devices in a mesh: groups: 2 (over x), tensor: 16 (over z, y, core).
Axes of the slice: x: 2, y: 2, z: 4, core: 2. Of those that a mesh axis runs over, the one named last changes fastest.
Arguments:
- resid: bfloat16 [128, 8192], P(('groups', 'tensor')), parts along dimension 0, may hold values from -6 to 6
- labels: int32 [128, 1], P(('groups', 'tensor')), parts along dimension 0, may hold values from 0 to 7
- erase_mean: float32 [8192], replicated, may hold values from -3 to 3
- erase_down: float32 [8192, 8], replicated, may hold values from -0.0625 to 0.0625
- erase_up: float32 [8, 8192], replicated, may hold values from -2 to 2
- norm_gain: float32 [8192], replicated, may hold values from 0.25 to 1.75
- w_gate: bfloat16 [8192, 14336], P(None, 'tensor'), may hold values from -0.0625 to 0.0625
- w_up: bfloat16 [8192, 14336], P(None, 'tensor'), may hold values from -0.0625 to 0.0625
- w_down: bfloat16 [14336, 8192], P('tensor'), may hold values from -0.046875 to 0.046875
Outputs:
- block_out: bfloat16 [128, 8192], P(('groups', 'tensor')), parts along dimension 0
- class_dev: float32 [16, 8192], P('groups', 'tensor'), parts along dimension 0
- covariance: bfloat16 [16384, 8192], P(('groups', 'tensor')), parts along dimension 0
The draws below stay inside these ranges and needn't reach their ends.
There are 2 independent parts, one for each index of `groups`. The reference program is written for one: setup_inputs(seed, part) draws one part's arguments, and reference() takes and returns one part's arrays. A program takes and returns all parts, laid end to end along the dimension named above; an argument that names none is the same for every part. Nothing has to cross between parts.
Inputs may be any that keep to these rules, and one draw needn't show every extreme that they name: Every class 0 to 7 labels at least one row of a group.
All inputs are finite; a program needn't handle non-finite values.
Results may differ from the reference program's by a relative error of at most 0.013.
Values may be sent and summed in bfloat16 or wider, within the bound.
A program may use at most 128 MiB of HBM per device.

```python
import jax
import jax.numpy as jnp
from jax import lax

D = 8192
FF = 14336
CLASSES = 8
ROWS = 64


def block_levels(rng, dims, split, low, high):
    loudness, own = 1.0, jax.random.fold_in(rng, 6)
    for axis_at, shards_of in split:
        heights = jnp.exp(jax.random.uniform(jax.random.fold_in(own, axis_at), (shards_of,), jnp.float32, low / len(split), high / len(split)))
        loudness = loudness * jnp.repeat(heights, dims[axis_at] // shards_of).reshape([-1 if axis == axis_at else 1 for axis in range(len(dims))])
    return loudness


def choose_distinct(rng, rows, number_of, top, lift):
    sequence = jax.random.permutation(jax.random.fold_in(rng, 1), number_of)
    pull = sequence
    for power in range(3):
        pull = pull * pull // number_of
    pull = pull * lift // number_of
    tickets = jax.random.randint(jax.random.fold_in(rng, 2), (rows, number_of), 0, 4096) + pull
    sure = jax.random.permutation(jax.random.fold_in(rng, 3), rows)[jnp.arange(number_of) % rows]
    tickets = jnp.where(jnp.arange(rows)[:, None] == sure[None, :], 1 << 14, tickets)
    score = tickets * number_of + jnp.arange(number_of)
    return lax.top_k(score.astype(jnp.int32), top)[1].astype(jnp.int32)


def gaussian(key, shape, width, bound, cuts=(), kind=jnp.bfloat16):
    gain = block_levels(key, shape, cuts, -0.22, 0.18) if cuts else 1.0
    values = jax.random.normal(key, shape, jnp.float32) * width * gain
    return jnp.minimum(jnp.maximum(values, -bound), bound).astype(kind)


def setup_inputs(seed: int = 0, part: int = 0) -> dict:
    keys = jax.random.split(jax.random.key(seed), 10)
    own_keys = jax.random.split(jax.random.fold_in(keys[9], part), 10)
    resid = gaussian(own_keys[0], (ROWS, D), 1.0, 6.0, ((0, 16),))
    labels = choose_distinct(own_keys[1], ROWS, CLASSES, 1, 0)
    erase_mean = gaussian(keys[2], (D,), 0.5, 3.0, (), jnp.float32)
    erase_down = gaussian(keys[3], (D, CLASSES), D ** -0.5, 0.0625, (), jnp.float32)
    erase_up = gaussian(keys[4], (CLASSES, D), 0.35, 2.0, (), jnp.float32)
    norm_gain = jnp.clip(1.0 + 0.15 * jax.random.normal(keys[5], (D,), jnp.float32), 0.25, 1.75)
    w_gate = gaussian(keys[6], (D, FF), D ** -0.5, 0.0625, ((1, 16),))
    w_up = gaussian(keys[7], (D, FF), D ** -0.5, 0.0625, ((1, 16),))
    w_down = gaussian(keys[8], (FF, D), FF ** -0.5, 0.046875, ((0, 16),))
    return {"resid": resid, "labels": labels, "erase_mean": erase_mean, "erase_down": erase_down, "erase_up": erase_up, "norm_gain": norm_gain, "w_gate": w_gate, "w_up": w_up, "w_down": w_down}


def reference(resid, labels, erase_mean, erase_down, erase_up, norm_gain, w_gate, w_up, w_down):
    hi = lax.Precision.HIGHEST
    x = resid.astype(jnp.float32)
    proj = jnp.dot(x - erase_mean, erase_down, precision=hi)
    scrubbed = (x - jnp.dot(proj, erase_up, precision=hi)).astype(jnp.bfloat16)
    xs = scrubbed.astype(jnp.float32)
    normed = (xs * lax.rsqrt(lax.optimization_barrier(jnp.mean(xs * xs, axis=1, keepdims=True)) + 1e-05) * norm_gain).astype(jnp.bfloat16)
    gate = jnp.dot(normed, w_gate, preferred_element_type=jnp.float32)
    up = jnp.dot(normed, w_up, preferred_element_type=jnp.float32)
    hidden = (jax.nn.silu(gate) * up).astype(jnp.bfloat16)
    block_out = (xs + jnp.dot(hidden, w_down, preferred_element_type=jnp.float32)).astype(jnp.bfloat16)
    yf = block_out.astype(jnp.float32)
    onehot = (labels[:, 0][:, None] == jnp.arange(CLASSES, dtype=jnp.int32)[None, :]).astype(jnp.float32)
    class_sums = jnp.dot(onehot.T, yf, precision=hi)
    counts = lax.optimization_barrier(jnp.sum(onehot, axis=0))
    mean = lax.optimization_barrier(jnp.sum(class_sums, axis=0)) / ROWS
    class_dev = class_sums / counts[:, None] - mean
    centred = (yf - mean).astype(jnp.bfloat16)
    covariance = (jnp.dot(centred.T, centred, preferred_element_type=jnp.float32) / ROWS).astype(jnp.bfloat16)
    return (block_out, class_dev, covariance)
```

```python
import functools

import jax
import jax.numpy as jnp
from jax import lax
from jax.experimental import pallas as pl
from jax.experimental.pallas import tpu as pltpu
from jax.sharding import PartitionSpec as P

CLASSES = 8
EPS = 1e-05
TILE = 16
LANES = 128
MIB = 1 << 20
Z, Y, C = 4, 2, 2


def place():
    me = lax.axis_index("tensor")
    return me, me // (Y * C), (me // C) % Y, me % C


def index_of(z, y, c):
    return (z * Y + y) * C + c


def at_rows(ref, block, rows):
    return ref.at[pl.ds(pl.multiple_of(block * rows, rows), rows)]


def remote(src, dst, send, recv, peer):
    return pltpu.make_async_remote_copy(
        src_ref=src,
        dst_ref=dst,
        send_sem=send,
        recv_sem=recv,
        device_id={"tensor": peer},
        device_id_type=pl.DeviceIdType.MESH,
    )


def all_gather(buf, rows, send, recv):
    me, z, y, c = place()
    sibling = index_of(z, y, 1 - c)
    across = index_of(z, 1 - y, c)
    started = []

    def push(block, peer):
        part = at_rows(buf, block, rows)
        copy = remote(part, part, send.at[len(started)], recv.at[block], peer)
        copy.start()
        started.append(copy)

    def await_block(block, peer):
        part = at_rows(buf, block, rows)
        remote(part, part, send.at[0], recv.at[block], peer).wait_recv()

    for dz in (2, 1, 3):
        push(me, index_of((z + dz) % Z, y, c))
    push(me, across)
    push(me, sibling)
    for dz in (1, 3, 2):
        block = index_of((z + dz) % Z, y, c)
        await_block(block, block)
        push(block, across)
        push(block, sibling)
    for dz in (0, 1, 3, 2):
        block = index_of((z + dz) % Z, 1 - y, c)
        await_block(block, across)
        push(block, sibling)
    for dz in (0, 1, 3, 2):
        for to in (y, 1 - y):
            await_block(index_of((z + dz) % Z, to, 1 - c), sibling)
    return started


def mlp_kernel(
    own_rows,
    block_ref,
    gain_ref,
    wg_hbm,
    wu_hbm,
    wd_hbm,
    y_hbm,
    lab_ref,
    xg,
    xs,
    xn,
    wg,
    wu,
    wd,
    gate,
    up,
    hidden,
    s_core,
    r_core,
    s_y,
    r_y,
    s_z,
    r_z,
    out,
    g_sem,
    u_sem,
    d_sem,
    ag1_send,
    ag1_recv,
    ag2_send,
    ag2_recv,
    core_send,
    core_recv,
    y_send,
    y_recv,
    z_send,
    z_recv,
    o_sem,
):
    n = Z * Y * C
    rows, depth = xs.shape
    width = depth // n
    quarters = TILE // own_rows
    cols = depth // quarters
    me, z, y, c = place()
    sibling = index_of(z, y, 1 - c)
    across = index_of(z, 1 - y, c)
    chunks = g_sem.shape[0]
    kc = depth // chunks

    def load_gate(k):
        part = pl.ds(pl.multiple_of(k * kc, kc), kc)
        return pltpu.make_async_copy(wg_hbm.at[part], wg.at[part], g_sem.at[k])

    def load_up(k):
        part = pl.ds(pl.multiple_of(k * kc, kc), kc)
        return pltpu.make_async_copy(wu_hbm.at[part], wu.at[part], u_sem.at[k])

    def load_down(pos, block):
        part = pl.ds(pl.multiple_of(block * width, width), width)
        return pltpu.make_async_copy(wd_hbm.at[:, part], wd.at[pos], d_sem.at[pos])

    order = (
        [index_of(k, 1 - y, 1 - c) for k in range(Z)]
        + [index_of(k, y, 1 - c) for k in range(Z)]
        + [index_of(k, 1 - y, c) for k in range(Z)]
        + [index_of((z + dz) % Z, y, c) for dz in (2, 1, 3)]
        + [me]
    )

    barrier = pltpu.get_barrier_semaphore()
    peers = [index_of((z + dz) % Z, y, c) for dz in (1, 2, 3)] + [across, sibling]
    for peer in peers:
        pl.semaphore_signal(
            barrier, inc=1, device_id={"tensor": peer}, device_id_type=pl.DeviceIdType.MESH
        )
    for k in range(chunks):
        load_gate(k).start()
        load_up(k).start()
    for pos in range(n):
        load_down(pos, order[pos]).start()
    own_part = pl.ds(pl.multiple_of(me * TILE, TILE), TILE)
    xg[own_part, :] = block_ref[...]
    pl.semaphore_wait(barrier, len(peers))

    started = all_gather(xg, TILE, ag1_send, ag1_recv)

    row = lax.broadcasted_iota(jnp.int32, (rows, n * TILE), 0)
    col = lax.broadcasted_iota(jnp.int32, (rows, n * TILE), 1)
    base = (row // own_rows) * TILE + row % own_rows
    picks = [
        jnp.where(col == base + q * own_rows, 1.0, 0.0).astype(jnp.bfloat16)
        for q in range(quarters)
    ]
    step = 512
    lab_ref[...] = jnp.dot(
        picks[0], xg[:, cols : cols + LANES], preferred_element_type=jnp.float32
    )

    def spread(i, total):
        at = pl.multiple_of(i * step, step)
        taken = xg[:, pl.ds(at, step)]
        for q in range(quarters):
            part = jnp.dot(picks[q], taken, preferred_element_type=jnp.float32)
            xs[:, pl.ds(pl.multiple_of(q * cols + at, step), step)] = part.astype(jnp.bfloat16)
            total = total + part * part
        return total

    total = lax.fori_loop(0, cols // step, spread, jnp.zeros((rows, step), jnp.float32))
    scale = lax.rsqrt(jnp.sum(total, axis=1, keepdims=True) / depth + EPS)

    def norm(i, carry):
        at = pl.ds(pl.multiple_of(i * step, step), step)
        xn[:, at] = (xs[:, at].astype(jnp.float32) * scale * gain_ref[:, at]).astype(jnp.bfloat16)
        return carry

    lax.fori_loop(0, depth // step, norm, 0)

    gate[...] = jnp.zeros_like(gate)
    up[...] = jnp.zeros_like(up)

    def project(k, carry):
        part = pl.ds(pl.multiple_of(k * kc, kc), kc)
        left = xn[:, part]
        load_gate(k).wait()
        gate[...] += jnp.dot(left, wg[part, :], preferred_element_type=jnp.float32)
        load_up(k).wait()
        up[...] += jnp.dot(left, wu[part, :], preferred_element_type=jnp.float32)
        return carry

    lax.fori_loop(0, chunks, project, 0)
    gated = gate[...]
    hidden[...] = (gated / (1.0 + jnp.exp(-gated)) * up[...]).astype(jnp.bfloat16)

    def share(pos, block):
        load_down(pos, block).wait()
        return jnp.dot(hidden[...], wd[pos], preferred_element_type=jnp.float32)

    def core_copy(k):
        return remote(s_core.at[k], r_core.at[k], core_send.at[k], core_recv.at[k], sibling)

    def y_copy(k):
        return remote(s_y.at[k], r_y.at[k], y_send.at[k], y_recv.at[k], across)

    def z_copy(dz):
        return remote(
            s_z.at[dz - 1],
            r_z.at[dz - 1],
            z_send.at[dz - 1],
            z_recv.at[dz - 1],
            index_of((z + dz) % Z, y, c),
        )

    def to_core(k, carry):
        block = index_of(k % Z, jnp.where(k < Z, 1 - y, y), 1 - c)
        s_core[k] = share(k, block).astype(jnp.bfloat16)
        core_copy(k).start()
        return carry

    lax.fori_loop(0, 2 * Z, to_core, 0)

    def to_y(k, carry):
        mine = share(2 * Z + k, index_of(k, 1 - y, c))
        core_copy(k).wait_recv()
        s_y[k] = (mine + r_core[k].astype(jnp.float32)).astype(jnp.bfloat16)
        y_copy(k).start()
        return carry

    lax.fori_loop(0, Z, to_y, 0)

    def chip_rows(pos, to):
        mine = share(pos, index_of(to, y, c))
        core_copy(Z + to).wait_recv()
        y_copy(to).wait_recv()
        return mine + r_core[Z + to].astype(jnp.float32) + r_y[to].astype(jnp.float32)

    for i, dz in enumerate((2, 1, 3)):
        s_z[dz - 1] = chip_rows(3 * Z + i, (z + dz) % Z).astype(jnp.bfloat16)
        z_copy(dz).start()
    summed = chip_rows(n - 1, z)
    for dz in (1, 3, 2):
        z_copy(dz).wait_recv()
        summed = summed + r_z[dz - 1].astype(jnp.float32)
    mine = pl.ds(pl.multiple_of(me * width, width), width)
    kept = (xs[:, mine].astype(jnp.float32) + summed).astype(jnp.bfloat16)
    out[pl.ds(pl.multiple_of(me * rows, rows), rows), :] = kept

    started += all_gather(out, rows, ag2_send, ag2_recv)
    store = pltpu.make_async_copy(out, y_hbm, o_sem)
    store.start()
    for copy in started:
        copy.wait_send()

    def finish(k, carry):
        core_copy(k).wait_send()
        return carry

    lax.fori_loop(0, 2 * Z, finish, 0)

    def finish_y(k, carry):
        y_copy(k).wait_send()
        return carry

    lax.fori_loop(0, Z, finish_y, 0)
    for dz in (1, 2, 3):
        z_copy(dz).wait_send()
    store.wait()


def stats_kernel(own_rows, y_ref, lab_ref, block_ref, dev_ref, cov_ref, owned):
    n = Z * Y * C
    rows = lab_ref.shape[0]
    step = pl.program_id(0)
    me = lax.axis_index("tensor")

    def centre(block):
        part = y_ref[pl.ds(pl.multiple_of(block * rows, rows), rows), :]
        full = part.astype(jnp.float32)
        mean = jnp.sum(full, axis=0, keepdims=True) / rows
        return part, mean, full - mean

    @pl.when(step == 0)
    def _():
        part, mean, dev = centre(me)
        owned[...] = dev.T.astype(jnp.bfloat16)
        lanes = lax.broadcasted_iota(jnp.int32, lab_ref.shape, 1).astype(jnp.float32)
        onehot = jnp.where(lab_ref[...] == lanes, 1.0, 0.0).astype(jnp.bfloat16)
        down = (((0,), (0,)), ((), ()))
        sums = lax.dot_general(onehot, part, down, preferred_element_type=jnp.float32)
        counts = lax.dot_general(
            onehot, jnp.ones_like(part), down, preferred_element_type=jnp.float32
        )
        dev_ref[...] = sums[:CLASSES] / counts[:CLASSES] - mean

    part, _, dev = centre(step)
    gram = jnp.dot(owned[...], dev.astype(jnp.bfloat16), preferred_element_type=jnp.float32)
    cov_ref[...] = (gram / rows).astype(jnp.bfloat16)
    row = lax.broadcasted_iota(jnp.int32, (TILE, rows), 0)
    col = lax.broadcasted_iota(jnp.int32, (TILE, rows), 1)
    pick = jnp.where(col == row + me * own_rows, 1.0, 0.0).astype(jnp.bfloat16)
    taken = jnp.dot(pick, part, preferred_element_type=jnp.float32)
    block_ref[...] = taken[:own_rows].astype(jnp.bfloat16)


def scrub(resid, erase_mean, erase_down, erase_up):
    highest = lax.Precision.HIGHEST
    x = resid.astype(jnp.float32)
    proj = jnp.dot(x - erase_mean, erase_down, precision=highest)
    return (x - jnp.dot(proj, erase_up, precision=highest)).astype(jnp.bfloat16)


def kernel_body(resid, labels, erase_mean, erase_down, erase_up, norm_gain, w_gate, w_up, w_down):
    n = Z * Y * C
    own_rows, depth = resid.shape
    rows, width, units = own_rows * n, depth // n, w_gate.shape[1]
    quarters = TILE // own_rows
    cols = depth // quarters
    scrubbed = scrub(resid, erase_mean, erase_down, erase_up)
    stacked = scrubbed.reshape(own_rows, quarters, cols).transpose(1, 0, 2).reshape(TILE, cols)
    tags = jnp.tile(jnp.broadcast_to(labels, (own_rows, LANES)), (quarters, 1))
    block = jnp.concatenate([stacked, tags.astype(jnp.bfloat16)], axis=1)

    chunks = 8
    bf16, f32 = jnp.bfloat16, jnp.float32
    vmem, hbm = pl.BlockSpec(memory_space=pltpu.VMEM), pl.BlockSpec(memory_space=pl.ANY)
    dma = pltpu.SemaphoreType.DMA
    weights = 3 * depth * units
    gathered, tagged = pl.pallas_call(
        functools.partial(mlp_kernel, own_rows),
        out_shape=(
            jax.ShapeDtypeStruct((n * rows, width), bf16),
            jax.ShapeDtypeStruct((rows, LANES), f32),
        ),
        in_specs=[vmem, vmem, hbm, hbm, hbm],
        out_specs=(hbm, vmem),
        scratch_shapes=[
            pltpu.VMEM((n * TILE, cols + LANES), bf16),
            pltpu.VMEM((rows, depth), bf16),
            pltpu.VMEM((rows, depth), bf16),
            pltpu.VMEM((depth, units), bf16),
            pltpu.VMEM((depth, units), bf16),
            pltpu.VMEM((n, units, width), bf16),
            pltpu.VMEM((rows, units), f32),
            pltpu.VMEM((rows, units), f32),
            pltpu.VMEM((rows, units), bf16),
            pltpu.VMEM((2 * Z, rows, width), bf16),
            pltpu.VMEM((2 * Z, rows, width), bf16),
            pltpu.VMEM((Z, rows, width), bf16),
            pltpu.VMEM((Z, rows, width), bf16),
            pltpu.VMEM((Z - 1, rows, width), bf16),
            pltpu.VMEM((Z - 1, rows, width), bf16),
            pltpu.VMEM((n * rows, width), bf16),
            dma((chunks,)),
            dma((chunks,)),
            dma((n,)),
            dma((n,)),
            dma((n,)),
            dma((n,)),
            dma((n,)),
            dma((2 * Z,)),
            dma((2 * Z,)),
            dma((Z,)),
            dma((Z,)),
            dma((Z - 1,)),
            dma((Z - 1,)),
            dma,
        ],
        compiler_params=pltpu.CompilerParams(
            collective_id=0, has_side_effects=True, vmem_limit_bytes=58 * MIB
        ),
        cost_estimate=pl.CostEstimate(
            flops=2 * rows * weights, bytes_accessed=2 * weights, transcendentals=rows * units
        ),
    )(block, norm_gain.reshape(1, depth), w_gate, w_up, w_down)

    return pl.pallas_call(
        functools.partial(stats_kernel, own_rows),
        grid=(n,),
        out_shape=(
            jax.ShapeDtypeStruct((own_rows, depth), bf16),
            jax.ShapeDtypeStruct((CLASSES, width), f32),
            jax.ShapeDtypeStruct((width, depth), bf16),
        ),
        in_specs=[vmem, vmem],
        out_specs=(
            pl.BlockSpec((own_rows, width), lambda j: (0, j)),
            pl.BlockSpec((CLASSES, width), lambda j: (0, 0)),
            pl.BlockSpec((width, width), lambda j: (0, j)),
        ),
        scratch_shapes=[pltpu.VMEM((width, rows), bf16)],
        compiler_params=pltpu.CompilerParams(vmem_limit_bytes=24 * MIB),
        cost_estimate=pl.CostEstimate(
            flops=2 * rows * width * depth, bytes_accessed=2 * width * depth, transcendentals=0
        ),
    )(gathered, tagged)


def plain_body(resid, labels, erase_mean, erase_down, erase_up, norm_gain, w_gate, w_up, w_down):
    ranks = lax.axis_size("tensor")
    own = lax.axis_index("tensor")
    total_rows = resid.shape[0] * ranks
    width = resid.shape[1] // ranks
    xs = scrub(resid, erase_mean, erase_down, erase_up).astype(jnp.float32)
    normed = (xs * lax.rsqrt(jnp.mean(xs * xs, axis=1, keepdims=True) + EPS) * norm_gain).astype(
        jnp.bfloat16
    )
    piece = lax.all_gather(normed, "tensor", axis=0, tiled=True)
    gate = jnp.dot(piece, w_gate, preferred_element_type=jnp.float32)
    up = jnp.dot(piece, w_up, preferred_element_type=jnp.float32)
    hidden = (jax.nn.silu(gate) * up).astype(jnp.bfloat16)
    summed = lax.psum_scatter(
        jnp.dot(hidden, w_down, preferred_element_type=jnp.float32),
        "tensor",
        scatter_dimension=0,
        tiled=True,
    )
    block_out = (xs + summed).astype(jnp.bfloat16)
    yf = block_out.astype(jnp.float32)
    onehot = (labels == jnp.arange(CLASSES, dtype=jnp.int32)[None, :]).astype(jnp.float32)
    class_sums, counts = lax.psum(
        (jnp.dot(onehot.T, yf, precision=lax.Precision.HIGHEST), jnp.sum(onehot, axis=0)), "tensor"
    )
    mean = jnp.sum(class_sums, axis=0) / total_rows
    deviation = class_sums / counts[:, None] - mean
    class_dev = lax.dynamic_slice_in_dim(deviation, own * width, width, 1)
    centred = (yf - mean).astype(jnp.bfloat16)
    piece = lax.all_gather(centred, "tensor", axis=0, tiled=True)
    owned = lax.dynamic_slice_in_dim(piece, own * width, width, 1)
    gram = lax.dot_general(
        owned, piece, (((0,), (0,)), ((), ())), preferred_element_type=jnp.float32
    )
    return block_out, class_dev, (gram / total_rows).astype(jnp.bfloat16)


def solution(mesh):
    body = kernel_body if mesh.shape["tensor"] == Z * Y * C else plain_body
    return jax.shard_map(
        body,
        mesh=mesh,
        in_specs=(
            P(("groups", "tensor"), None),
            P(("groups", "tensor"), None),
            P(),
            P(),
            P(),
            P(),
            P(None, "tensor"),
            P(None, "tensor"),
            P("tensor", None),
        ),
        out_specs=(
            P(("groups", "tensor"), None),
            P("groups", "tensor"),
            P(("groups", "tensor"), None),
        ),
        check_vma=False,
    )
```

```python
import functools

import jax
import jax.numpy as jnp
from jax import lax
from jax.experimental import pallas as pl
from jax.experimental.pallas import tpu as pltpu
from jax.sharding import PartitionSpec as P

CLASSES = 8
EPS = 1e-05
TILE = 16
LANES = 128
MIB = 1 << 20
GROUP = 2
Z, Y, C = 4, 2, 2


def place():
    me = lax.axis_index("tensor")
    return me, me // (Y * C), (me // C) % Y, me % C


def index_of(z, y, c):
    return (z * Y + y) * C + c


def at_rows(ref, block, rows):
    return ref.at[pl.ds(pl.multiple_of(block * rows, rows), rows)]


def far_first(z):
    low = z < Z // 2
    return [jnp.where(low, 3, 0), jnp.where(low, 2, 1), jnp.where(low, 1 - z, 5 - z)]


def remote(src, dst, send, recv, peer):
    return pltpu.make_async_remote_copy(
        src_ref=src,
        dst_ref=dst,
        send_sem=send,
        recv_sem=recv,
        device_id={"tensor": peer},
        device_id_type=pl.DeviceIdType.MESH,
    )


def all_gather(buf, rows, send, recv):
    me, z, y, c = place()
    sibling = index_of(z, y, 1 - c)
    across = index_of(z, 1 - y, c)
    started = []

    def push(block, peer):
        part = at_rows(buf, block, rows)
        copy = remote(part, part, send.at[len(started)], recv.at[block], peer)
        copy.start()
        started.append(copy)

    def await_block(block, peer):
        part = at_rows(buf, block, rows)
        remote(part, part, send.at[0], recv.at[block], peer).wait_recv()

    others = far_first(z)
    for to in others:
        push(me, index_of(to, y, c))
    push(me, across)
    push(me, sibling)
    for to in others:
        block = index_of(to, y, c)
        await_block(block, block)
        push(block, across)
        push(block, sibling)
    for to in [z] + others:
        block = index_of(to, 1 - y, c)
        await_block(block, across)
        push(block, sibling)
    for to in range(Z):
        for line in (y, 1 - y):
            await_block(index_of(to, line, 1 - c), sibling)
    return started


def mlp_kernel(
    own_rows,
    resid_ref,
    labels_ref,
    mean_ref,
    down_ref,
    up_ref,
    gain_ref,
    wg_hbm,
    wu_hbm,
    wd_hbm,
    y_hbm,
    own_ref,
    lab_ref,
    stack,
    xg,
    xs,
    xn,
    wg,
    wu,
    wd,
    gate,
    up,
    hidden,
    s_core,
    r_core,
    s_y,
    r_y,
    s_z,
    r_z,
    out,
    g_sem,
    u_sem,
    d_sem,
    ag1_send,
    ag1_recv,
    ag2_send,
    ag2_recv,
    core_send,
    core_recv,
    y_send,
    y_recv,
    z_send,
    z_recv,
    o_sem,
):
    n = Z * Y * C
    rows, depth = xs.shape
    width = depth // n
    quarters = TILE // own_rows
    cols = depth // quarters
    me, z, y, c = place()
    sibling = index_of(z, y, 1 - c)
    across = index_of(z, 1 - y, c)
    chunks = g_sem.shape[0]
    kc = depth // chunks

    def load_gate(k):
        part = pl.ds(pl.multiple_of(k * kc, kc), kc)
        return pltpu.make_async_copy(wg_hbm.at[part], wg.at[part], g_sem.at[k])

    def load_up(k):
        part = pl.ds(pl.multiple_of(k * kc, kc), kc)
        return pltpu.make_async_copy(wu_hbm.at[part], wu.at[part], u_sem.at[k])

    def load_down(pos, block):
        part = pl.ds(pl.multiple_of(block * width, width), width)
        return pltpu.make_async_copy(wd_hbm.at[:, part], wd.at[pos], d_sem.at[pos])

    turns = far_first(z) + [z]

    def turn(k):
        low = z < Z // 2
        third = jnp.where(low, 1 - z, 5 - z)
        two = jnp.where(low, 3 - k, k)
        return jnp.where(k == 3, z, jnp.where(k == 2, third, two))

    order = [
        index_of(to, line, core)
        for line, core in ((1 - y, 1 - c), (y, 1 - c), (1 - y, c), (y, c))
        for to in turns
    ]

    barrier = pltpu.get_barrier_semaphore()
    peers = [index_of((z + dz) % Z, y, c) for dz in (1, 2, 3)] + [across, sibling]
    for peer in peers:
        pl.semaphore_signal(
            barrier, inc=1, device_id={"tensor": peer}, device_id_type=pl.DeviceIdType.MESH
        )
    for k in range(chunks):
        load_gate(k).start()
        load_up(k).start()
    for pos in range(n):
        load_down(pos, order[pos]).start()

    x = resid_ref[...].astype(jnp.float32)
    from_mean = x - mean_ref[...]
    erased = jnp.zeros_like(x)
    for i in range(CLASSES):
        proj = jnp.sum(from_mean * down_ref[i : i + 1, :], axis=1, keepdims=True)
        erased = erased + proj * up_ref[i : i + 1, :]
    scrubbed = x - erased
    tags = jnp.broadcast_to(labels_ref[...].astype(jnp.float32), (own_rows, LANES))
    for q in range(quarters):
        stack[q * own_rows : (q + 1) * own_rows, :cols] = scrubbed[:, q * cols : (q + 1) * cols]
        stack[q * own_rows : (q + 1) * own_rows, cols:] = tags
    xg[pl.ds(pl.multiple_of(me * TILE, TILE), TILE), :] = stack[...].astype(jnp.bfloat16)
    pl.semaphore_wait(barrier, len(peers))

    started = all_gather(xg, TILE, ag1_send, ag1_recv)

    row = lax.broadcasted_iota(jnp.int32, (rows, n * TILE), 0)
    col = lax.broadcasted_iota(jnp.int32, (rows, n * TILE), 1)
    base = (row // own_rows) * TILE + row % own_rows
    picks = [
        jnp.where(col == base + q * own_rows, 1.0, 0.0).astype(jnp.bfloat16)
        for q in range(quarters)
    ]
    step = 512
    lab_ref[...] = jnp.dot(
        picks[0], xg[:, cols : cols + LANES], preferred_element_type=jnp.float32
    )

    def spread(i, total):
        at = pl.multiple_of(i * step, step)
        taken = xg[:, pl.ds(at, step)]
        for q in range(quarters):
            part = jnp.dot(picks[q], taken, preferred_element_type=jnp.float32)
            xs[:, pl.ds(pl.multiple_of(q * cols + at, step), step)] = part.astype(jnp.bfloat16)
            total = total + part * part
        return total

    total = lax.fori_loop(0, cols // step, spread, jnp.zeros((rows, step), jnp.float32))
    scale = lax.rsqrt(jnp.sum(total, axis=1, keepdims=True) / depth + EPS)

    def norm(i, carry):
        at = pl.ds(pl.multiple_of(i * step, step), step)
        xn[:, at] = (xs[:, at].astype(jnp.float32) * scale * gain_ref[:, at]).astype(jnp.bfloat16)
        return carry

    lax.fori_loop(0, depth // step, norm, 0)

    gate[...] = jnp.zeros_like(gate)
    up[...] = jnp.zeros_like(up)

    def project(k, carry):
        part = pl.ds(pl.multiple_of(k * kc, kc), kc)
        left = xn[:, part]
        load_gate(k).wait()
        gate[...] += jnp.dot(left, wg[part, :], preferred_element_type=jnp.float32)
        load_up(k).wait()
        up[...] += jnp.dot(left, wu[part, :], preferred_element_type=jnp.float32)
        return carry

    lax.fori_loop(0, chunks, project, 0)
    gated = gate[...]
    hidden[...] = (gated / (1.0 + jnp.exp(-gated)) * up[...]).astype(jnp.bfloat16)

    def share(pos, block):
        load_down(pos, block).wait()
        return jnp.dot(hidden[...], wd[pos], preferred_element_type=jnp.float32)

    def core_copy(k):
        return remote(s_core.at[k], r_core.at[k], core_send.at[k], core_recv.at[k], sibling)

    def y_copy(k):
        return remote(s_y.at[k], r_y.at[k], y_send.at[k], y_recv.at[k], across)

    def z_copy(to):
        slot = (to - z + Z) % Z - 1
        return remote(
            s_z.at[slot], r_z.at[slot], z_send.at[slot], z_recv.at[slot], index_of(to, y, c)
        )

    def to_core(k, carry):
        block = index_of(turn(k % Z), jnp.where(k < Z, 1 - y, y), 1 - c)
        s_core[k] = share(k, block).astype(jnp.bfloat16)
        core_copy(k).start()
        return carry

    lax.fori_loop(0, 2 * Z, to_core, 0)

    def to_y(k, carry):
        mine = share(2 * Z + k, index_of(turn(k), 1 - y, c))
        core_copy(k).wait_recv()
        s_y[k] = (mine + r_core[k].astype(jnp.float32)).astype(jnp.bfloat16)
        y_copy(k).start()
        return carry

    lax.fori_loop(0, Z, to_y, 0)

    def chip_rows(k):
        mine = share(3 * Z + k, index_of(turns[k], y, c))
        core_copy(Z + k).wait_recv()
        y_copy(k).wait_recv()
        return mine + r_core[Z + k].astype(jnp.float32) + r_y[k].astype(jnp.float32)

    for k in range(Z - 1):
        s_z[(turns[k] - z + Z) % Z - 1] = chip_rows(k).astype(jnp.bfloat16)
        z_copy(turns[k]).start()
    summed = chip_rows(Z - 1)
    for dz in range(1, Z):
        z_copy((z + dz) % Z).wait_recv()
        summed = summed + r_z[dz - 1].astype(jnp.float32)
    mine = pl.ds(pl.multiple_of(me * width, width), width)
    kept = (xs[:, mine].astype(jnp.float32) + summed).astype(jnp.bfloat16)
    out[pl.ds(pl.multiple_of(me * rows, rows), rows), :] = kept
    own_ref[...] = kept

    started += all_gather(out, rows, ag2_send, ag2_recv)
    store = pltpu.make_async_copy(out, y_hbm, o_sem)
    store.start()
    for copy in started:
        copy.wait_send()

    def finish(k, carry):
        core_copy(k).wait_send()
        return carry

    lax.fori_loop(0, 2 * Z, finish, 0)

    def finish_y(k, carry):
        y_copy(k).wait_send()
        return carry

    lax.fori_loop(0, Z, finish_y, 0)
    for dz in range(1, Z):
        z_copy((z + dz) % Z).wait_send()
    store.wait()


def stats_kernel(own_rows, y_ref, own_ref, lab_ref, block_ref, dev_ref, cov_ref, owned):
    rows, width = own_ref.shape
    me = lax.axis_index("tensor")

    def centre(part):
        full = part.astype(jnp.float32)
        mean = jnp.sum(full, axis=0, keepdims=True) * (1.0 / rows)
        return mean, full - mean

    @pl.when(pl.program_id(0) == 0)
    def _():
        part = own_ref[...]
        mean, dev = centre(part)
        owned[...] = dev.T.astype(jnp.bfloat16)
        lanes = lax.broadcasted_iota(jnp.int32, lab_ref.shape, 1).astype(jnp.float32)
        onehot = jnp.where(lab_ref[...] == lanes, 1.0, 0.0).astype(jnp.bfloat16)
        down = (((0,), (0,)), ((), ()))
        sums = lax.dot_general(onehot, part, down, preferred_element_type=jnp.float32)
        counts = lax.dot_general(
            onehot, jnp.ones_like(part), down, preferred_element_type=jnp.float32
        )
        dev_ref[...] = sums[:CLASSES] / counts[:CLASSES] - mean

    row = lax.broadcasted_iota(jnp.int32, (TILE, rows), 0)
    col = lax.broadcasted_iota(jnp.int32, (TILE, rows), 1)
    pick = jnp.where(col == row + me * own_rows, 1.0, 0.0).astype(jnp.bfloat16)
    for i in range(GROUP):
        at = slice(i * width, (i + 1) * width)
        part = y_ref[i * rows : (i + 1) * rows, :]
        _, dev = centre(part)
        gram = jnp.dot(owned[...], dev.astype(jnp.bfloat16), preferred_element_type=jnp.float32)
        cov_ref[:, at] = (gram * (1.0 / rows)).astype(jnp.bfloat16)
        taken = jnp.dot(pick, part, preferred_element_type=jnp.float32)
        block_ref[:, at] = taken[:own_rows].astype(jnp.bfloat16)


def scrub(resid, erase_mean, erase_down, erase_up):
    highest = lax.Precision.HIGHEST
    x = resid.astype(jnp.float32)
    proj = jnp.dot(x - erase_mean, erase_down, precision=highest)
    return (x - jnp.dot(proj, erase_up, precision=highest)).astype(jnp.bfloat16)


def kernel_body(resid, labels, erase_mean, erase_down, erase_up, norm_gain, w_gate, w_up, w_down):
    n = Z * Y * C
    own_rows, depth = resid.shape
    rows, width, units = own_rows * n, depth // n, w_gate.shape[1]
    quarters = TILE // own_rows
    cols = depth // quarters
    chunks = 8
    bf16, f32 = jnp.bfloat16, jnp.float32
    vmem, hbm = pl.BlockSpec(memory_space=pltpu.VMEM), pl.BlockSpec(memory_space=pl.ANY)
    dma = pltpu.SemaphoreType.DMA
    weights = 3 * depth * units
    gathered, owned, tagged = pl.pallas_call(
        functools.partial(mlp_kernel, own_rows),
        out_shape=(
            jax.ShapeDtypeStruct((n * rows, width), bf16),
            jax.ShapeDtypeStruct((rows, width), bf16),
            jax.ShapeDtypeStruct((rows, LANES), f32),
        ),
        in_specs=[vmem] * 6 + [hbm] * 3,
        out_specs=(hbm, vmem, vmem),
        scratch_shapes=[
            pltpu.VMEM((TILE, cols + LANES), f32),
            pltpu.VMEM((n * TILE, cols + LANES), bf16),
            pltpu.VMEM((rows, depth), bf16),
            pltpu.VMEM((rows, depth), bf16),
            pltpu.VMEM((depth, units), bf16),
            pltpu.VMEM((depth, units), bf16),
            pltpu.VMEM((n, units, width), bf16),
            pltpu.VMEM((rows, units), f32),
            pltpu.VMEM((rows, units), f32),
            pltpu.VMEM((rows, units), bf16),
            pltpu.VMEM((2 * Z, rows, width), bf16),
            pltpu.VMEM((2 * Z, rows, width), bf16),
            pltpu.VMEM((Z, rows, width), bf16),
            pltpu.VMEM((Z, rows, width), bf16),
            pltpu.VMEM((Z - 1, rows, width), bf16),
            pltpu.VMEM((Z - 1, rows, width), bf16),
            pltpu.VMEM((n * rows, width), bf16),
            dma((chunks,)),
            dma((chunks,)),
            dma((n,)),
            dma((n,)),
            dma((n,)),
            dma((n,)),
            dma((n,)),
            dma((2 * Z,)),
            dma((2 * Z,)),
            dma((Z,)),
            dma((Z,)),
            dma((Z - 1,)),
            dma((Z - 1,)),
            dma,
        ],
        compiler_params=pltpu.CompilerParams(
            collective_id=0, has_side_effects=True, vmem_limit_bytes=58 * MIB
        ),
        cost_estimate=pl.CostEstimate(
            flops=2 * rows * weights, bytes_accessed=2 * weights, transcendentals=rows * units
        ),
    )(
        resid,
        labels,
        erase_mean.reshape(1, depth),
        erase_down.T,
        erase_up,
        norm_gain.reshape(1, depth),
        w_gate,
        w_up,
        w_down,
    )

    return pl.pallas_call(
        functools.partial(stats_kernel, own_rows),
        grid=(n // GROUP,),
        out_shape=(
            jax.ShapeDtypeStruct((own_rows, depth), bf16),
            jax.ShapeDtypeStruct((CLASSES, width), f32),
            jax.ShapeDtypeStruct((width, depth), bf16),
        ),
        in_specs=[
            pl.BlockSpec((GROUP * rows, width), lambda j: (j, 0)),
            pl.BlockSpec((rows, width), lambda j: (0, 0)),
            pl.BlockSpec((rows, LANES), lambda j: (0, 0)),
        ],
        out_specs=(
            pl.BlockSpec((own_rows, GROUP * width), lambda j: (0, j)),
            pl.BlockSpec((CLASSES, width), lambda j: (0, 0)),
            pl.BlockSpec((width, GROUP * width), lambda j: (0, j)),
        ),
        scratch_shapes=[pltpu.VMEM((width, rows), bf16)],
        compiler_params=pltpu.CompilerParams(vmem_limit_bytes=24 * MIB),
        cost_estimate=pl.CostEstimate(
            flops=2 * rows * width * depth, bytes_accessed=2 * width * depth, transcendentals=0
        ),
    )(gathered, owned, tagged)


def plain_body(resid, labels, erase_mean, erase_down, erase_up, norm_gain, w_gate, w_up, w_down):
    ranks = lax.axis_size("tensor")
    own = lax.axis_index("tensor")
    total_rows = resid.shape[0] * ranks
    width = resid.shape[1] // ranks
    xs = scrub(resid, erase_mean, erase_down, erase_up).astype(jnp.float32)
    normed = (xs * lax.rsqrt(jnp.mean(xs * xs, axis=1, keepdims=True) + EPS) * norm_gain).astype(
        jnp.bfloat16
    )
    piece = lax.all_gather(normed, "tensor", axis=0, tiled=True)
    gate = jnp.dot(piece, w_gate, preferred_element_type=jnp.float32)
    up = jnp.dot(piece, w_up, preferred_element_type=jnp.float32)
    hidden = (jax.nn.silu(gate) * up).astype(jnp.bfloat16)
    summed = lax.psum_scatter(
        jnp.dot(hidden, w_down, preferred_element_type=jnp.float32),
        "tensor",
        scatter_dimension=0,
        tiled=True,
    )
    block_out = (xs + summed).astype(jnp.bfloat16)
    yf = block_out.astype(jnp.float32)
    onehot = (labels == jnp.arange(CLASSES, dtype=jnp.int32)[None, :]).astype(jnp.float32)
    class_sums, counts = lax.psum(
        (jnp.dot(onehot.T, yf, precision=lax.Precision.HIGHEST), jnp.sum(onehot, axis=0)), "tensor"
    )
    mean = jnp.sum(class_sums, axis=0) / total_rows
    deviation = class_sums / counts[:, None] - mean
    class_dev = lax.dynamic_slice_in_dim(deviation, own * width, width, 1)
    centred = (yf - mean).astype(jnp.bfloat16)
    piece = lax.all_gather(centred, "tensor", axis=0, tiled=True)
    owned = lax.dynamic_slice_in_dim(piece, own * width, width, 1)
    gram = lax.dot_general(
        owned, piece, (((0,), (0,)), ((), ())), preferred_element_type=jnp.float32
    )
    return block_out, class_dev, (gram / total_rows).astype(jnp.bfloat16)


def solution(mesh):
    body = kernel_body if mesh.shape["tensor"] == Z * Y * C else plain_body
    return jax.shard_map(
        body,
        mesh=mesh,
        in_specs=(
            P(("groups", "tensor"), None),
            P(("groups", "tensor"), None),
            P(),
            P(),
            P(),
            P(),
            P(None, "tensor"),
            P(None, "tensor"),
            P("tensor", None),
        ),
        out_specs=(
            P(("groups", "tensor"), None),
            P("groups", "tensor"),
            P(("groups", "tensor"), None),
        ),
        check_vma=False,
    )
```

```python
import functools

import jax
import jax.numpy as jnp
from jax import lax
from jax.experimental import pallas as pl
from jax.experimental.pallas import tpu as pltpu
from jax.sharding import PartitionSpec as P

CLASSES = 8
EPS = 1e-05
TILE = 16
LANES = 128
MIB = 1 << 20
GROUP = 4
Z, Y, C = 4, 2, 2


def place():
    me = lax.axis_index("tensor")
    return me, me // (Y * C), (me // C) % Y, me % C


def index_of(z, y, c):
    return (z * Y + y) * C + c


def at_rows(ref, block, rows):
    return ref.at[pl.ds(pl.multiple_of(block * rows, rows), rows)]


def far_first(z):
    low = z < Z // 2
    return [jnp.where(low, 3, 0), jnp.where(low, 2, 1), jnp.where(low, 1 - z, 5 - z)]


def remote(src, dst, send, recv, peer):
    return pltpu.make_async_remote_copy(
        src_ref=src,
        dst_ref=dst,
        send_sem=send,
        recv_sem=recv,
        device_id={"tensor": peer},
        device_id_type=pl.DeviceIdType.MESH,
    )


def all_gather(buf, rows, send, recv):
    me, z, y, c = place()
    sibling = index_of(z, y, 1 - c)
    across = index_of(z, 1 - y, c)
    started = []

    def push(block, peer):
        part = at_rows(buf, block, rows)
        copy = remote(part, part, send.at[len(started)], recv.at[block], peer)
        copy.start()
        started.append(copy)

    def await_block(block, peer):
        part = at_rows(buf, block, rows)
        remote(part, part, send.at[0], recv.at[block], peer).wait_recv()

    others = far_first(z)
    for to in others:
        push(me, index_of(to, y, c))
    push(me, across)
    push(me, sibling)
    for to in others:
        block = index_of(to, y, c)
        await_block(block, block)
        push(block, across)
        push(block, sibling)
    for to in [z] + others:
        block = index_of(to, 1 - y, c)
        await_block(block, across)
        push(block, sibling)
    for to in range(Z):
        for line in (y, 1 - y):
            await_block(index_of(to, line, 1 - c), sibling)
    return started


def mlp_kernel(
    own_rows,
    resid_ref,
    labels_ref,
    mean_ref,
    down_ref,
    up_ref,
    gain_ref,
    wg_hbm,
    wu_hbm,
    wd_hbm,
    y_hbm,
    own_ref,
    lab_ref,
    stack,
    xg,
    xs,
    xn,
    wg,
    wu,
    wd,
    gate,
    up,
    hidden,
    s_core,
    r_core,
    s_y,
    r_y,
    s_z,
    r_z,
    out,
    g_sem,
    u_sem,
    d_sem,
    ag1_send,
    ag1_recv,
    ag2_send,
    ag2_recv,
    core_send,
    core_recv,
    y_send,
    y_recv,
    z_send,
    z_recv,
    o_sem,
):
    n = Z * Y * C
    rows, depth = xs.shape
    width = depth // n
    quarters = TILE // own_rows
    cols = depth // quarters
    me, z, y, c = place()
    sibling = index_of(z, y, 1 - c)
    across = index_of(z, 1 - y, c)
    chunks = g_sem.shape[0]
    kc = depth // chunks

    def load_gate(k):
        part = pl.ds(pl.multiple_of(k * kc, kc), kc)
        return pltpu.make_async_copy(wg_hbm.at[part], wg.at[part], g_sem.at[k])

    def load_up(k):
        part = pl.ds(pl.multiple_of(k * kc, kc), kc)
        return pltpu.make_async_copy(wu_hbm.at[part], wu.at[part], u_sem.at[k])

    def load_down(pos, block):
        part = pl.ds(pl.multiple_of(block * width, width), width)
        return pltpu.make_async_copy(wd_hbm.at[:, part], wd.at[pos], d_sem.at[pos])

    turns = far_first(z) + [z]

    def turn(k):
        low = z < Z // 2
        third = jnp.where(low, 1 - z, 5 - z)
        two = jnp.where(low, 3 - k, k)
        return jnp.where(k == 3, z, jnp.where(k == 2, third, two))

    order = [
        index_of(to, line, core)
        for line, core in ((1 - y, 1 - c), (y, 1 - c), (1 - y, c), (y, c))
        for to in turns
    ]

    barrier = pltpu.get_barrier_semaphore()
    peers = [index_of((z + dz) % Z, y, c) for dz in (1, 2, 3)] + [across, sibling]
    for peer in peers:
        pl.semaphore_signal(
            barrier, inc=1, device_id={"tensor": peer}, device_id_type=pl.DeviceIdType.MESH
        )
    for k in range(chunks):
        load_gate(k).start()
        load_up(k).start()
    for pos in range(n):
        load_down(pos, order[pos]).start()

    x = resid_ref[...].astype(jnp.float32)
    from_mean = x - mean_ref[...]
    erased = jnp.zeros_like(x)
    for i in range(CLASSES):
        proj = jnp.sum(from_mean * down_ref[i : i + 1, :], axis=1, keepdims=True)
        erased = erased + proj * up_ref[i : i + 1, :]
    scrubbed = x - erased
    down = lax.broadcasted_iota(jnp.int32, (own_rows, own_rows), 0)
    right = lax.broadcasted_iota(jnp.int32, (own_rows, own_rows), 1)
    label_row = jnp.broadcast_to(labels_ref[...].astype(jnp.float32), (own_rows, own_rows))
    label_column = jnp.sum(jnp.where(down == right, label_row, 0.0), axis=1, keepdims=True)
    tags = jnp.broadcast_to(label_column, (own_rows, LANES))
    for q in range(quarters):
        stack[q * own_rows : (q + 1) * own_rows, :cols] = scrubbed[:, q * cols : (q + 1) * cols]
        stack[q * own_rows : (q + 1) * own_rows, cols:] = tags
    xg[pl.ds(pl.multiple_of(me * TILE, TILE), TILE), :] = stack[...].astype(jnp.bfloat16)
    pl.semaphore_wait(barrier, len(peers))

    started = all_gather(xg, TILE, ag1_send, ag1_recv)

    row = lax.broadcasted_iota(jnp.int32, (rows, n * TILE), 0)
    col = lax.broadcasted_iota(jnp.int32, (rows, n * TILE), 1)
    base = (row // own_rows) * TILE + row % own_rows
    picks = [
        jnp.where(col == base + q * own_rows, 1.0, 0.0).astype(jnp.bfloat16)
        for q in range(quarters)
    ]
    step = 512
    lab_ref[...] = jnp.dot(
        picks[0], xg[:, cols : cols + LANES], preferred_element_type=jnp.float32
    )

    def spread(i, total):
        at = pl.multiple_of(i * step, step)
        taken = xg[:, pl.ds(at, step)]
        for q in range(quarters):
            part = jnp.dot(picks[q], taken, preferred_element_type=jnp.float32)
            xs[:, pl.ds(pl.multiple_of(q * cols + at, step), step)] = part.astype(jnp.bfloat16)
            total = total + part * part
        return total

    total = lax.fori_loop(0, cols // step, spread, jnp.zeros((rows, step), jnp.float32))
    scale = lax.rsqrt(jnp.sum(total, axis=1, keepdims=True) / depth + EPS)

    def norm(i, carry):
        at = pl.ds(pl.multiple_of(i * step, step), step)
        xn[:, at] = (xs[:, at].astype(jnp.float32) * scale * gain_ref[:, at]).astype(jnp.bfloat16)
        return carry

    lax.fori_loop(0, depth // step, norm, 0)

    gate[...] = jnp.zeros_like(gate)
    up[...] = jnp.zeros_like(up)

    def project(k, carry):
        part = pl.ds(pl.multiple_of(k * kc, kc), kc)
        left = xn[:, part]
        load_gate(k).wait()
        gate[...] += jnp.dot(left, wg[part, :], preferred_element_type=jnp.float32)
        load_up(k).wait()
        up[...] += jnp.dot(left, wu[part, :], preferred_element_type=jnp.float32)
        return carry

    lax.fori_loop(0, chunks, project, 0)
    gated = gate[...]
    hidden[...] = (gated / (1.0 + jnp.exp(-gated)) * up[...]).astype(jnp.bfloat16)

    def share(pos, block):
        load_down(pos, block).wait()
        return jnp.dot(hidden[...], wd[pos], preferred_element_type=jnp.float32)

    def core_copy(k):
        return remote(s_core.at[k], r_core.at[k], core_send.at[k], core_recv.at[k], sibling)

    def y_copy(k):
        return remote(s_y.at[k], r_y.at[k], y_send.at[k], y_recv.at[k], across)

    def z_copy(to):
        slot = (to - z + Z) % Z - 1
        return remote(
            s_z.at[slot], r_z.at[slot], z_send.at[slot], z_recv.at[slot], index_of(to, y, c)
        )

    def to_core(k, carry):
        block = index_of(turn(k % Z), jnp.where(k < Z, 1 - y, y), 1 - c)
        s_core[k] = share(k, block).astype(jnp.bfloat16)
        core_copy(k).start()
        return carry

    lax.fori_loop(0, 2 * Z, to_core, 0)

    def to_y(k, carry):
        mine = share(2 * Z + k, index_of(turn(k), 1 - y, c))
        core_copy(k).wait_recv()
        s_y[k] = (mine + r_core[k].astype(jnp.float32)).astype(jnp.bfloat16)
        y_copy(k).start()
        return carry

    lax.fori_loop(0, Z, to_y, 0)

    def chip_rows(k):
        mine = share(3 * Z + k, index_of(turns[k], y, c))
        core_copy(Z + k).wait_recv()
        y_copy(k).wait_recv()
        return mine + r_core[Z + k].astype(jnp.float32) + r_y[k].astype(jnp.float32)

    for k in range(Z - 1):
        s_z[(turns[k] - z + Z) % Z - 1] = chip_rows(k).astype(jnp.bfloat16)
        z_copy(turns[k]).start()
    summed = chip_rows(Z - 1)
    for dz in range(1, Z):
        z_copy((z + dz) % Z).wait_recv()
        summed = summed + r_z[dz - 1].astype(jnp.float32)
    mine = pl.ds(pl.multiple_of(me * width, width), width)
    kept = (xs[:, mine].astype(jnp.float32) + summed).astype(jnp.bfloat16)
    out[pl.ds(pl.multiple_of(me * rows, rows), rows), :] = kept
    own_ref[...] = kept

    started += all_gather(out, rows, ag2_send, ag2_recv)
    store = pltpu.make_async_copy(out, y_hbm, o_sem)
    store.start()
    for copy in started:
        copy.wait_send()

    def finish(k, carry):
        core_copy(k).wait_send()
        return carry

    lax.fori_loop(0, 2 * Z, finish, 0)

    def finish_y(k, carry):
        y_copy(k).wait_send()
        return carry

    lax.fori_loop(0, Z, finish_y, 0)
    for dz in range(1, Z):
        z_copy((z + dz) % Z).wait_send()
    store.wait()


def stats_kernel(own_rows, y_ref, own_ref, lab_ref, block_ref, dev_ref, cov_ref, owned):
    rows, width = own_ref.shape
    me = lax.axis_index("tensor")

    def centre(part):
        full = part.astype(jnp.float32)
        mean = jnp.sum(full, axis=0, keepdims=True) * (1.0 / rows)
        return mean, full - mean

    @pl.when(pl.program_id(0) == 0)
    def _():
        part = own_ref[...]
        mean, dev = centre(part)
        owned[...] = dev.T.astype(jnp.bfloat16)
        lanes = lax.broadcasted_iota(jnp.int32, lab_ref.shape, 1).astype(jnp.float32)
        onehot = jnp.where(lab_ref[...] == lanes, 1.0, 0.0).astype(jnp.bfloat16)
        down = (((0,), (0,)), ((), ()))
        sums = lax.dot_general(onehot, part, down, preferred_element_type=jnp.float32)
        counts = lax.dot_general(
            onehot, jnp.ones_like(part), down, preferred_element_type=jnp.float32
        )
        dev_ref[...] = sums[:CLASSES] / counts[:CLASSES] - mean

    row = lax.broadcasted_iota(jnp.int32, (TILE, rows), 0)
    col = lax.broadcasted_iota(jnp.int32, (TILE, rows), 1)
    pick = jnp.where(col == row + me * own_rows, 1.0, 0.0).astype(jnp.bfloat16)
    for i in range(GROUP):
        at = slice(i * width, (i + 1) * width)
        part = y_ref[i * rows : (i + 1) * rows, :]
        _, dev = centre(part)
        gram = jnp.dot(owned[...], dev.astype(jnp.bfloat16), preferred_element_type=jnp.float32)
        cov_ref[:, at] = (gram * (1.0 / rows)).astype(jnp.bfloat16)
        taken = jnp.dot(pick, part, preferred_element_type=jnp.float32)
        block_ref[:, at] = taken[:own_rows].astype(jnp.bfloat16)


def scrub(resid, erase_mean, erase_down, erase_up):
    highest = lax.Precision.HIGHEST
    x = resid.astype(jnp.float32)
    proj = jnp.dot(x - erase_mean, erase_down, precision=highest)
    return (x - jnp.dot(proj, erase_up, precision=highest)).astype(jnp.bfloat16)


def kernel_body(resid, labels, erase_mean, erase_down, erase_up, norm_gain, w_gate, w_up, w_down):
    n = Z * Y * C
    own_rows, depth = resid.shape
    rows, width, units = own_rows * n, depth // n, w_gate.shape[1]
    quarters = TILE // own_rows
    cols = depth // quarters
    chunks = 8
    bf16, f32 = jnp.bfloat16, jnp.float32
    vmem, hbm = pl.BlockSpec(memory_space=pltpu.VMEM), pl.BlockSpec(memory_space=pl.ANY)
    dma = pltpu.SemaphoreType.DMA
    weights = 3 * depth * units
    gathered, owned, tagged = pl.pallas_call(
        functools.partial(mlp_kernel, own_rows),
        out_shape=(
            jax.ShapeDtypeStruct((n * rows, width), bf16),
            jax.ShapeDtypeStruct((rows, width), bf16),
            jax.ShapeDtypeStruct((rows, LANES), f32),
        ),
        in_specs=[vmem] * 6 + [hbm] * 3,
        out_specs=(hbm, vmem, vmem),
        scratch_shapes=[
            pltpu.VMEM((TILE, cols + LANES), f32),
            pltpu.VMEM((n * TILE, cols + LANES), bf16),
            pltpu.VMEM((rows, depth), bf16),
            pltpu.VMEM((rows, depth), bf16),
            pltpu.VMEM((depth, units), bf16),
            pltpu.VMEM((depth, units), bf16),
            pltpu.VMEM((n, units, width), bf16),
            pltpu.VMEM((rows, units), f32),
            pltpu.VMEM((rows, units), f32),
            pltpu.VMEM((rows, units), bf16),
            pltpu.VMEM((2 * Z, rows, width), bf16),
            pltpu.VMEM((2 * Z, rows, width), bf16),
            pltpu.VMEM((Z, rows, width), bf16),
            pltpu.VMEM((Z, rows, width), bf16),
            pltpu.VMEM((Z - 1, rows, width), bf16),
            pltpu.VMEM((Z - 1, rows, width), bf16),
            pltpu.VMEM((n * rows, width), bf16),
            dma((chunks,)),
            dma((chunks,)),
            dma((n,)),
            dma((n,)),
            dma((n,)),
            dma((n,)),
            dma((n,)),
            dma((2 * Z,)),
            dma((2 * Z,)),
            dma((Z,)),
            dma((Z,)),
            dma((Z - 1,)),
            dma((Z - 1,)),
            dma,
        ],
        compiler_params=pltpu.CompilerParams(
            collective_id=0, has_side_effects=True, vmem_limit_bytes=58 * MIB
        ),
        cost_estimate=pl.CostEstimate(
            flops=2 * rows * weights, bytes_accessed=2 * weights, transcendentals=rows * units
        ),
    )(
        resid,
        labels.T,
        erase_mean.reshape(1, depth),
        erase_down.T,
        erase_up,
        norm_gain.reshape(1, depth),
        w_gate,
        w_up,
        w_down,
    )

    return pl.pallas_call(
        functools.partial(stats_kernel, own_rows),
        grid=(n // GROUP,),
        out_shape=(
            jax.ShapeDtypeStruct((own_rows, depth), bf16),
            jax.ShapeDtypeStruct((CLASSES, width), f32),
            jax.ShapeDtypeStruct((width, depth), bf16),
        ),
        in_specs=[
            pl.BlockSpec((GROUP * rows, width), lambda j: (j, 0)),
            pl.BlockSpec((rows, width), lambda j: (0, 0)),
            pl.BlockSpec((rows, LANES), lambda j: (0, 0)),
        ],
        out_specs=(
            pl.BlockSpec((own_rows, GROUP * width), lambda j: (0, j)),
            pl.BlockSpec((CLASSES, width), lambda j: (0, 0)),
            pl.BlockSpec((width, GROUP * width), lambda j: (0, j)),
        ),
        scratch_shapes=[pltpu.VMEM((width, rows), bf16)],
        compiler_params=pltpu.CompilerParams(vmem_limit_bytes=58 * MIB),
        cost_estimate=pl.CostEstimate(
            flops=2 * rows * width * depth, bytes_accessed=2 * width * depth, transcendentals=0
        ),
    )(gathered, owned, tagged)


def plain_body(resid, labels, erase_mean, erase_down, erase_up, norm_gain, w_gate, w_up, w_down):
    ranks = lax.axis_size("tensor")
    own = lax.axis_index("tensor")
    total_rows = resid.shape[0] * ranks
    width = resid.shape[1] // ranks
    xs = scrub(resid, erase_mean, erase_down, erase_up).astype(jnp.float32)
    normed = (xs * lax.rsqrt(jnp.mean(xs * xs, axis=1, keepdims=True) + EPS) * norm_gain).astype(
        jnp.bfloat16
    )
    piece = lax.all_gather(normed, "tensor", axis=0, tiled=True)
    gate = jnp.dot(piece, w_gate, preferred_element_type=jnp.float32)
    up = jnp.dot(piece, w_up, preferred_element_type=jnp.float32)
    hidden = (jax.nn.silu(gate) * up).astype(jnp.bfloat16)
    summed = lax.psum_scatter(
        jnp.dot(hidden, w_down, preferred_element_type=jnp.float32),
        "tensor",
        scatter_dimension=0,
        tiled=True,
    )
    block_out = (xs + summed).astype(jnp.bfloat16)
    yf = block_out.astype(jnp.float32)
    onehot = (labels == jnp.arange(CLASSES, dtype=jnp.int32)[None, :]).astype(jnp.float32)
    class_sums, counts = lax.psum(
        (jnp.dot(onehot.T, yf, precision=lax.Precision.HIGHEST), jnp.sum(onehot, axis=0)), "tensor"
    )
    mean = jnp.sum(class_sums, axis=0) / total_rows
    deviation = class_sums / counts[:, None] - mean
    class_dev = lax.dynamic_slice_in_dim(deviation, own * width, width, 1)
    centred = (yf - mean).astype(jnp.bfloat16)
    piece = lax.all_gather(centred, "tensor", axis=0, tiled=True)
    owned = lax.dynamic_slice_in_dim(piece, own * width, width, 1)
    gram = lax.dot_general(
        owned, piece, (((0,), (0,)), ((), ())), preferred_element_type=jnp.float32
    )
    return block_out, class_dev, (gram / total_rows).astype(jnp.bfloat16)


def solution(mesh):
    body = kernel_body if mesh.shape["tensor"] == Z * Y * C else plain_body
    return jax.shard_map(
        body,
        mesh=mesh,
        in_specs=(
            P(("groups", "tensor"), None),
            P(("groups", "tensor"), None),
            P(),
            P(),
            P(),
            P(),
            P(None, "tensor"),
            P(None, "tensor"),
            P("tensor", None),
        ),
        out_specs=(
            P(("groups", "tensor"), None),
            P("groups", "tensor"),
            P(("groups", "tensor"), None),
        ),
        check_vma=False,
    )
```

```python
import functools

import jax
import jax.numpy as jnp
from jax import lax
from jax.experimental import pallas as pl
from jax.experimental.pallas import tpu as pltpu
from jax.sharding import PartitionSpec as P

CLASSES = 8
EPS = 1e-05
TILE = 16
LANES = 128
MIB = 1 << 20
GROUP = 4
Z, Y, C = 4, 2, 2


def place():
    me = lax.axis_index("tensor")
    return me, me // (Y * C), (me // C) % Y, me % C


def index_of(z, y, c):
    return (z * Y + y) * C + c


def at_rows(ref, block, rows):
    return ref.at[pl.ds(pl.multiple_of(block * rows, rows), rows)]


def far_first(z):
    low = z < Z // 2
    return [jnp.where(low, 3, 0), jnp.where(low, 2, 1), jnp.where(low, 1 - z, 5 - z)]


def remote(src, dst, send, recv, peer):
    return pltpu.make_async_remote_copy(
        src_ref=src,
        dst_ref=dst,
        send_sem=send,
        recv_sem=recv,
        device_id={"tensor": peer},
        device_id_type=pl.DeviceIdType.MESH,
    )


def all_gather(buf, rows, send, recv):
    me, z, y, c = place()
    sibling = index_of(z, y, 1 - c)
    across = index_of(z, 1 - y, c)
    started = []

    def push(block, peer):
        part = at_rows(buf, block, rows)
        copy = remote(part, part, send.at[len(started)], recv.at[block], peer)
        copy.start()
        started.append(copy)

    def await_block(block, peer):
        part = at_rows(buf, block, rows)
        remote(part, part, send.at[0], recv.at[block], peer).wait_recv()

    others = far_first(z)
    push(me, across)
    for to in others:
        push(me, index_of(to, y, c))
    push(me, sibling)
    for to in others:
        block = index_of(to, y, c)
        await_block(block, block)
        push(block, across)
        push(block, sibling)
    for to in [z] + others:
        block = index_of(to, 1 - y, c)
        await_block(block, across)
        push(block, sibling)
    for to in range(Z):
        for line in (y, 1 - y):
            await_block(index_of(to, line, 1 - c), sibling)
    return started


def mlp_kernel(
    own_rows,
    resid_ref,
    labels_ref,
    mean_ref,
    down_ref,
    up_ref,
    gain_ref,
    wg_hbm,
    wu_hbm,
    wd_hbm,
    y_hbm,
    own_ref,
    lab_ref,
    stack,
    xg,
    xs,
    xn,
    wg,
    wu,
    wd,
    gate,
    up,
    hidden,
    s_core,
    r_core,
    s_y,
    r_y,
    s_z,
    r_z,
    out,
    g_sem,
    u_sem,
    d_sem,
    ag1_send,
    ag1_recv,
    ag2_send,
    ag2_recv,
    core_send,
    core_recv,
    y_send,
    y_recv,
    z_send,
    z_recv,
    o_sem,
):
    n = Z * Y * C
    rows, depth = xs.shape
    width = depth // n
    quarters = TILE // own_rows
    cols = depth // quarters
    me, z, y, c = place()
    sibling = index_of(z, y, 1 - c)
    across = index_of(z, 1 - y, c)
    chunks = g_sem.shape[0]
    kc = depth // chunks

    def load_gate(k):
        part = pl.ds(pl.multiple_of(k * kc, kc), kc)
        return pltpu.make_async_copy(wg_hbm.at[part], wg.at[part], g_sem.at[k])

    def load_up(k):
        part = pl.ds(pl.multiple_of(k * kc, kc), kc)
        return pltpu.make_async_copy(wu_hbm.at[part], wu.at[part], u_sem.at[k])

    def load_down(pos, block):
        part = pl.ds(pl.multiple_of(block * width, width), width)
        return pltpu.make_async_copy(wd_hbm.at[:, part], wd.at[pos], d_sem.at[pos])

    turns = far_first(z) + [z]

    def turn(k):
        low = z < Z // 2
        third = jnp.where(low, 1 - z, 5 - z)
        two = jnp.where(low, 3 - k, k)
        return jnp.where(k == 3, z, jnp.where(k == 2, third, two))

    order = [
        index_of(to, line, core)
        for line, core in ((1 - y, 1 - c), (y, 1 - c), (1 - y, c), (y, c))
        for to in turns
    ]

    barrier = pltpu.get_barrier_semaphore()
    peers = [index_of((z + dz) % Z, y, c) for dz in (1, 2, 3)] + [across, sibling]
    for peer in peers:
        pl.semaphore_signal(
            barrier, inc=1, device_id={"tensor": peer}, device_id_type=pl.DeviceIdType.MESH
        )
    for k in range(chunks):
        load_gate(k).start()
        load_up(k).start()
    for pos in range(n):
        load_down(pos, order[pos]).start()

    x = resid_ref[...].astype(jnp.float32)
    from_mean = x - mean_ref[...]
    erased = jnp.zeros_like(x)
    for i in range(CLASSES):
        proj = jnp.sum(from_mean * down_ref[i : i + 1, :], axis=1, keepdims=True)
        erased = erased + proj * up_ref[i : i + 1, :]
    scrubbed = x - erased
    down = lax.broadcasted_iota(jnp.int32, (own_rows, own_rows), 0)
    right = lax.broadcasted_iota(jnp.int32, (own_rows, own_rows), 1)
    label_row = jnp.broadcast_to(labels_ref[...].astype(jnp.float32), (own_rows, own_rows))
    label_column = jnp.sum(jnp.where(down == right, label_row, 0.0), axis=1, keepdims=True)
    tags = jnp.broadcast_to(label_column, (own_rows, LANES))
    for q in range(quarters):
        stack[q * own_rows : (q + 1) * own_rows, :cols] = scrubbed[:, q * cols : (q + 1) * cols]
        stack[q * own_rows : (q + 1) * own_rows, cols:] = tags
    xg[pl.ds(pl.multiple_of(me * TILE, TILE), TILE), :] = stack[...].astype(jnp.bfloat16)
    pl.semaphore_wait(barrier, len(peers))

    started = all_gather(xg, TILE, ag1_send, ag1_recv)

    row = lax.broadcasted_iota(jnp.int32, (rows, n * TILE), 0)
    col = lax.broadcasted_iota(jnp.int32, (rows, n * TILE), 1)
    base = (row // own_rows) * TILE + row % own_rows
    picks = [
        jnp.where(col == base + q * own_rows, 1.0, 0.0).astype(jnp.bfloat16)
        for q in range(quarters)
    ]
    step = 512
    lab_ref[...] = jnp.dot(
        picks[0], xg[:, cols : cols + LANES], preferred_element_type=jnp.float32
    )

    def spread(i, total):
        at = pl.multiple_of(i * step, step)
        taken = xg[:, pl.ds(at, step)]
        for q in range(quarters):
            part = jnp.dot(picks[q], taken, preferred_element_type=jnp.float32)
            xs[:, pl.ds(pl.multiple_of(q * cols + at, step), step)] = part.astype(jnp.bfloat16)
            total = total + part * part
        return total

    total = lax.fori_loop(0, cols // step, spread, jnp.zeros((rows, step), jnp.float32))
    scale = lax.rsqrt(jnp.sum(total, axis=1, keepdims=True) / depth + EPS)

    def norm(i, carry):
        at = pl.ds(pl.multiple_of(i * step, step), step)
        xn[:, at] = (xs[:, at].astype(jnp.float32) * scale * gain_ref[:, at]).astype(jnp.bfloat16)
        return carry

    lax.fori_loop(0, depth // step, norm, 0)

    gate[...] = jnp.zeros_like(gate)
    up[...] = jnp.zeros_like(up)

    def project(k, carry):
        part = pl.ds(pl.multiple_of(k * kc, kc), kc)
        left = xn[:, part]
        load_gate(k).wait()
        gate[...] += jnp.dot(left, wg[part, :], preferred_element_type=jnp.float32)
        load_up(k).wait()
        up[...] += jnp.dot(left, wu[part, :], preferred_element_type=jnp.float32)
        return carry

    lax.fori_loop(0, chunks, project, 0)
    gated = gate[...]
    hidden[...] = (gated / (1.0 + jnp.exp(-gated)) * up[...]).astype(jnp.bfloat16)

    def share(pos, block):
        load_down(pos, block).wait()
        return jnp.dot(hidden[...], wd[pos], preferred_element_type=jnp.float32)

    def core_copy(k):
        return remote(s_core.at[k], r_core.at[k], core_send.at[k], core_recv.at[k], sibling)

    def y_copy(k):
        return remote(s_y.at[k], r_y.at[k], y_send.at[k], y_recv.at[k], across)

    def z_copy(to):
        slot = (to - z + Z) % Z - 1
        return remote(
            s_z.at[slot], r_z.at[slot], z_send.at[slot], z_recv.at[slot], index_of(to, y, c)
        )

    def to_core(k, carry):
        block = index_of(turn(k % Z), jnp.where(k < Z, 1 - y, y), 1 - c)
        s_core[k] = share(k, block).astype(jnp.bfloat16)
        core_copy(k).start()
        return carry

    lax.fori_loop(0, 2 * Z, to_core, 0)

    def to_y(k, carry):
        mine = share(2 * Z + k, index_of(turn(k), 1 - y, c))
        core_copy(k).wait_recv()
        s_y[k] = (mine + r_core[k].astype(jnp.float32)).astype(jnp.bfloat16)
        y_copy(k).start()
        return carry

    lax.fori_loop(0, Z, to_y, 0)

    def chip_rows(k):
        mine = share(3 * Z + k, index_of(turns[k], y, c))
        core_copy(Z + k).wait_recv()
        y_copy(k).wait_recv()
        return mine + r_core[Z + k].astype(jnp.float32) + r_y[k].astype(jnp.float32)

    for k in range(Z - 1):
        s_z[(turns[k] - z + Z) % Z - 1] = chip_rows(k).astype(jnp.bfloat16)
        z_copy(turns[k]).start()
    summed = chip_rows(Z - 1)
    for dz in range(1, Z):
        z_copy((z + dz) % Z).wait_recv()
        summed = summed + r_z[dz - 1].astype(jnp.float32)
    mine = pl.ds(pl.multiple_of(me * width, width), width)
    kept = (xs[:, mine].astype(jnp.float32) + summed).astype(jnp.bfloat16)
    out[pl.ds(pl.multiple_of(me * rows, rows), rows), :] = kept
    own_ref[...] = kept

    started += all_gather(out, rows, ag2_send, ag2_recv)
    store = pltpu.make_async_copy(out, y_hbm, o_sem)
    store.start()
    for copy in started:
        copy.wait_send()

    def finish(k, carry):
        core_copy(k).wait_send()
        return carry

    lax.fori_loop(0, 2 * Z, finish, 0)

    def finish_y(k, carry):
        y_copy(k).wait_send()
        return carry

    lax.fori_loop(0, Z, finish_y, 0)
    for dz in range(1, Z):
        z_copy((z + dz) % Z).wait_send()
    store.wait()


def stats_kernel(own_rows, y_ref, own_ref, lab_ref, block_ref, dev_ref, cov_ref, owned):
    rows, width = own_ref.shape
    me = lax.axis_index("tensor")

    def centre(part):
        full = part.astype(jnp.float32)
        mean = jnp.sum(full, axis=0, keepdims=True) * (1.0 / rows)
        return mean, full - mean

    @pl.when(pl.program_id(0) == 0)
    def _():
        part = own_ref[...]
        mean, dev = centre(part)
        owned[...] = dev.T.astype(jnp.bfloat16)
        lanes = lax.broadcasted_iota(jnp.int32, lab_ref.shape, 1).astype(jnp.float32)
        onehot = jnp.where(lab_ref[...] == lanes, 1.0, 0.0).astype(jnp.bfloat16)
        down = (((0,), (0,)), ((), ()))
        sums = lax.dot_general(onehot, part, down, preferred_element_type=jnp.float32)
        counts = lax.dot_general(
            onehot, jnp.ones_like(part), down, preferred_element_type=jnp.float32
        )
        dev_ref[...] = sums[:CLASSES] / counts[:CLASSES] - mean

    row = lax.broadcasted_iota(jnp.int32, (TILE, rows), 0)
    col = lax.broadcasted_iota(jnp.int32, (TILE, rows), 1)
    pick = jnp.where(col == row + me * own_rows, 1.0, 0.0).astype(jnp.bfloat16)
    for i in range(GROUP):
        at = slice(i * width, (i + 1) * width)
        part = y_ref[i * rows : (i + 1) * rows, :]
        _, dev = centre(part)
        gram = jnp.dot(owned[...], dev.astype(jnp.bfloat16), preferred_element_type=jnp.float32)
        cov_ref[:, at] = (gram * (1.0 / rows)).astype(jnp.bfloat16)
        taken = jnp.dot(pick, part, preferred_element_type=jnp.float32)
        block_ref[:, at] = taken[:own_rows].astype(jnp.bfloat16)


def scrub(resid, erase_mean, erase_down, erase_up):
    highest = lax.Precision.HIGHEST
    x = resid.astype(jnp.float32)
    proj = jnp.dot(x - erase_mean, erase_down, precision=highest)
    return (x - jnp.dot(proj, erase_up, precision=highest)).astype(jnp.bfloat16)


def kernel_body(resid, labels, erase_mean, erase_down, erase_up, norm_gain, w_gate, w_up, w_down):
    n = Z * Y * C
    own_rows, depth = resid.shape
    rows, width, units = own_rows * n, depth // n, w_gate.shape[1]
    quarters = TILE // own_rows
    cols = depth // quarters
    chunks = 8
    bf16, f32 = jnp.bfloat16, jnp.float32
    vmem, hbm = pl.BlockSpec(memory_space=pltpu.VMEM), pl.BlockSpec(memory_space=pl.ANY)
    dma = pltpu.SemaphoreType.DMA
    weights = 3 * depth * units
    gathered, owned, tagged = pl.pallas_call(
        functools.partial(mlp_kernel, own_rows),
        out_shape=(
            jax.ShapeDtypeStruct((n * rows, width), bf16),
            jax.ShapeDtypeStruct((rows, width), bf16),
            jax.ShapeDtypeStruct((rows, LANES), f32),
        ),
        in_specs=[vmem] * 6 + [hbm] * 3,
        out_specs=(hbm, vmem, vmem),
        scratch_shapes=[
            pltpu.VMEM((TILE, cols + LANES), f32),
            pltpu.VMEM((n * TILE, cols + LANES), bf16),
            pltpu.VMEM((rows, depth), bf16),
            pltpu.VMEM((rows, depth), bf16),
            pltpu.VMEM((depth, units), bf16),
            pltpu.VMEM((depth, units), bf16),
            pltpu.VMEM((n, units, width), bf16),
            pltpu.VMEM((rows, units), f32),
            pltpu.VMEM((rows, units), f32),
            pltpu.VMEM((rows, units), bf16),
            pltpu.VMEM((2 * Z, rows, width), bf16),
            pltpu.VMEM((2 * Z, rows, width), bf16),
            pltpu.VMEM((Z, rows, width), bf16),
            pltpu.VMEM((Z, rows, width), bf16),
            pltpu.VMEM((Z - 1, rows, width), bf16),
            pltpu.VMEM((Z - 1, rows, width), bf16),
            pltpu.VMEM((n * rows, width), bf16),
            dma((chunks,)),
            dma((chunks,)),
            dma((n,)),
            dma((n,)),
            dma((n,)),
            dma((n,)),
            dma((n,)),
            dma((2 * Z,)),
            dma((2 * Z,)),
            dma((Z,)),
            dma((Z,)),
            dma((Z - 1,)),
            dma((Z - 1,)),
            dma,
        ],
        compiler_params=pltpu.CompilerParams(
            collective_id=0, has_side_effects=True, vmem_limit_bytes=58 * MIB
        ),
        cost_estimate=pl.CostEstimate(
            flops=2 * rows * weights, bytes_accessed=2 * weights, transcendentals=rows * units
        ),
    )(
        resid,
        labels.T,
        erase_mean.reshape(1, depth),
        erase_down.T,
        erase_up,
        norm_gain.reshape(1, depth),
        w_gate,
        w_up,
        w_down,
    )

    return pl.pallas_call(
        functools.partial(stats_kernel, own_rows),
        grid=(n // GROUP,),
        out_shape=(
            jax.ShapeDtypeStruct((own_rows, depth), bf16),
            jax.ShapeDtypeStruct((CLASSES, width), f32),
            jax.ShapeDtypeStruct((width, depth), bf16),
        ),
        in_specs=[
            pl.BlockSpec((GROUP * rows, width), lambda j: (j, 0)),
            pl.BlockSpec((rows, width), lambda j: (0, 0)),
            pl.BlockSpec((rows, LANES), lambda j: (0, 0)),
        ],
        out_specs=(
            pl.BlockSpec((own_rows, GROUP * width), lambda j: (0, j)),
            pl.BlockSpec((CLASSES, width), lambda j: (0, 0)),
            pl.BlockSpec((width, GROUP * width), lambda j: (0, j)),
        ),
        scratch_shapes=[pltpu.VMEM((width, rows), bf16)],
        compiler_params=pltpu.CompilerParams(vmem_limit_bytes=58 * MIB),
        cost_estimate=pl.CostEstimate(
            flops=2 * rows * width * depth, bytes_accessed=2 * width * depth, transcendentals=0
        ),
    )(gathered, owned, tagged)


def plain_body(resid, labels, erase_mean, erase_down, erase_up, norm_gain, w_gate, w_up, w_down):
    ranks = lax.axis_size("tensor")
    own = lax.axis_index("tensor")
    total_rows = resid.shape[0] * ranks
    width = resid.shape[1] // ranks
    xs = scrub(resid, erase_mean, erase_down, erase_up).astype(jnp.float32)
    normed = (xs * lax.rsqrt(jnp.mean(xs * xs, axis=1, keepdims=True) + EPS) * norm_gain).astype(
        jnp.bfloat16
    )
    piece = lax.all_gather(normed, "tensor", axis=0, tiled=True)
    gate = jnp.dot(piece, w_gate, preferred_element_type=jnp.float32)
    up = jnp.dot(piece, w_up, preferred_element_type=jnp.float32)
    hidden = (jax.nn.silu(gate) * up).astype(jnp.bfloat16)
    summed = lax.psum_scatter(
        jnp.dot(hidden, w_down, preferred_element_type=jnp.float32),
        "tensor",
        scatter_dimension=0,
        tiled=True,
    )
    block_out = (xs + summed).astype(jnp.bfloat16)
    yf = block_out.astype(jnp.float32)
    onehot = (labels == jnp.arange(CLASSES, dtype=jnp.int32)[None, :]).astype(jnp.float32)
    class_sums, counts = lax.psum(
        (jnp.dot(onehot.T, yf, precision=lax.Precision.HIGHEST), jnp.sum(onehot, axis=0)), "tensor"
    )
    mean = jnp.sum(class_sums, axis=0) / total_rows
    deviation = class_sums / counts[:, None] - mean
    class_dev = lax.dynamic_slice_in_dim(deviation, own * width, width, 1)
    centred = (yf - mean).astype(jnp.bfloat16)
    piece = lax.all_gather(centred, "tensor", axis=0, tiled=True)
    owned = lax.dynamic_slice_in_dim(piece, own * width, width, 1)
    gram = lax.dot_general(
        owned, piece, (((0,), (0,)), ((), ())), preferred_element_type=jnp.float32
    )
    return block_out, class_dev, (gram / total_rows).astype(jnp.bfloat16)


def solution(mesh):
    body = kernel_body if mesh.shape["tensor"] == Z * Y * C else plain_body
    return jax.shard_map(
        body,
        mesh=mesh,
        in_specs=(
            P(("groups", "tensor"), None),
            P(("groups", "tensor"), None),
            P(),
            P(),
            P(),
            P(),
            P(None, "tensor"),
            P(None, "tensor"),
            P("tensor", None),
        ),
        out_specs=(
            P(("groups", "tensor"), None),
            P("groups", "tensor"),
            P(("groups", "tensor"), None),
        ),
        check_vma=False,
    )
```
